32 devices in a mesh: grp: 2 (over y), term: 4 (over z), batch: 2 (over x), sub: 2 (over core).
Axes of the slice: x: 2, y: 2, z: 4, core: 2. Of those that a mesh axis runs over, the one named last changes fastest.
Arguments:
- query_logits: bfloat16 [256, 151936], P(('grp', 'batch', 'sub'), 'term'), parts along dimension 0, may hold values from -8 to 8
- doc_logits: bfloat16 [1024, 151936], P(('grp', 'batch', 'sub'), 'term'), parts along dimension 0, may hold values from -8 to 8
- score_grad: bfloat16 [256, 512], P(('grp', 'term'), ('batch', 'sub')), parts along dimension 0, may hold values from -0.3984375 to 0.3984375
Outputs:
- query_logit_grad: bfloat16 [256, 151936], P(('grp', 'batch', 'sub'), 'term'), parts along dimension 0
- doc_logit_grad: bfloat16 [1024, 151936], P(('grp', 'batch', 'sub'), 'term'), parts along dimension 0
The draws below stay inside these ranges and needn't reach their ends.
There are 2 independent parts, one for each index of `grp`. The reference program is written for one: setup_inputs(seed, part) draws one part's arguments, and reference() takes and returns one part's arrays. A program takes and returns all parts, laid end to end along the dimension named above; each array names one. Nothing has to cross between parts.
All inputs are finite; a program needn't handle non-finite values.
Results may differ from the reference program's by a relative error of at most 0.01.
Values may be sent and summed in bfloat16 or wider, within the bound.
A program may use at most 192 MiB of HBM per device.

```python
import jax
import jax.numpy as jnp
from jax import lax

V = 151936
NQ = 128
ND = 512


def logit_field(key, row_count, col_count):
    first = jax.random.fold_in(key, 0)
    noise = jax.random.normal(first, (row_count, col_count), jnp.float32)
    rising = 0.5 + jnp.arange(row_count, dtype=jnp.float32) / (row_count - 1)
    values = noise * rising[:, None] - 0.2
    return jnp.clip(values, -8.0, 8.0)


def draw_query_logits(key, part):
    key = jax.random.fold_in(key, 11)
    values = logit_field(key, NQ, V)
    return values.astype(jnp.bfloat16)


def draw_doc_logits(key, part):
    key = jax.random.fold_in(key, 23)
    values = logit_field(key, ND, V)
    return values.astype(jnp.bfloat16)


def levels(rng, extent, pieces, smallest, largest):
    gain, own = 1.0, jax.random.fold_in(rng, 6)
    for axis_at, shards_of in pieces:
        draws = jnp.exp(jax.random.uniform(jax.random.fold_in(own, axis_at), (shards_of,), jnp.float32, smallest / len(pieces), largest / len(pieces)))
        gain = gain * jnp.repeat(draws, extent[axis_at] // shards_of).reshape([-1 if axis == axis_at else 1 for axis in range(len(extent))])
    return gain


def centred(key, extent, scale, most, pieces=(), kind=jnp.bfloat16):
    values = jax.random.normal(key, extent, jnp.float32) * scale
    if len(pieces) > 0:
        values = levels(key, extent, pieces, -0.22, 0.18) * values
    return jnp.clip(values, min=-most, max=most).astype(kind)


def setup_inputs(seed: int = 0, part: int = 0) -> dict:
    splits = jax.random.split(jax.random.key(seed), 4)
    part_splits = jax.random.split(jax.random.fold_in(splits[3], part), 4)
    query_logits = draw_query_logits(jax.random.fold_in(jax.random.fold_in(splits[3], part), 71), part)
    doc_logits = draw_doc_logits(jax.random.fold_in(jax.random.fold_in(splits[3], part), 71), part)
    score_grad = centred(part_splits[2], (NQ, ND), 0.06, 0.3984375, ((0, 4), (1, 4)))
    return dict(query_logits=query_logits, doc_logits=doc_logits, score_grad=score_grad)


query_reg = 1.0
doc_reg = 0.6


def impacts(logits):
    return jnp.log1p(jnp.maximum(logits.astype(jnp.float32), 0.0)).astype(jnp.bfloat16)


def saturate_back(grad, logits):
    values = logits.astype(jnp.float32)
    scaled = grad / (1.0 + jnp.maximum(values, 0.0))
    return jnp.where(values > 0.0, scaled, 0.0).astype(jnp.bfloat16)


def reference(query_logits, doc_logits, score_grad):
    query_impact = impacts(query_logits)
    doc_impact = impacts(doc_logits)
    query_mean = jnp.sum(query_impact, axis=0, dtype=jnp.float32) / NQ
    doc_mean = jnp.sum(doc_impact, axis=0, dtype=jnp.float32) / ND
    query_grad = jnp.dot(score_grad, doc_impact, preferred_element_type=jnp.float32)
    query_grad = query_grad + 2.0 * query_reg * query_mean[None, :]
    doc_grad = lax.dot_general(score_grad, query_impact, (((0,), (0,)), ((), ())), preferred_element_type=jnp.float32)
    doc_grad = doc_grad + 2.0 * doc_reg * doc_mean[None, :]
    return saturate_back(query_grad, query_logits), saturate_back(doc_grad, doc_logits)
```

```python
import functools

import jax
import jax.numpy as jnp
from jax import lax
from jax.experimental import pallas as pl
from jax.experimental.pallas import tpu as pltpu
from jax.sharding import PartitionSpec as P

query_reg = 1.0
doc_reg = 0.6

LANES = 128
CHUNK_TILES = 11
FORWARD_LAG = 2
OUT_LAG = 3
MESH = pl.DeviceIdType.MESH


def impacts(logits):
    return jnp.log1p(jnp.maximum(logits.astype(jnp.float32), 0.0)).astype(jnp.bfloat16)


def saturate_back(grad, logits):
    values = logits.astype(jnp.float32)
    scaled = grad / (1.0 + jnp.maximum(values, 0.0))
    return jnp.where(values > 0.0, scaled, 0.0).astype(jnp.bfloat16)


def kernel(
    chips, terms, chunks, num_queries, num_docs,
    score_ref, q_in, d_in, q_again, d_again, q_out, d_out,
    score_all, score_keep_send, score_t,
    q_all, p_keep, p_send, p_recv, x_send, x_recv, s_own, s_recv, s_chip, s_far,
    sc_ss, sc_rs, qs_ss, qs_rs, qx_ss, qx_rs, qf_ss, qf_rs,
    p_ss, p_rs, x_ss, x_rs, s_ss, s_rs, sx_ss, sx_rs,
):
    step = pl.program_id(0)
    rows = q_in.shape[0]
    term = lax.axis_index("term")
    chip = lax.axis_index("batch")
    core = lax.axis_index("sub")
    other = 1 - core
    sibling = {"sub": other}
    block = chip * 2 + core

    def chip_up(k):
        return lax.rem(chip + k, chips)

    def chip_down(k):
        return lax.rem(chip + chips - k, chips)

    def remote(src, dst, send, recv, device):
        return pltpu.make_async_remote_copy(
            src_ref=src, dst_ref=dst, send_sem=send, recv_sem=recv,
            device_id=device, device_id_type=MESH,
        )

    def score_copy(k):
        return remote(
            score_all.at[term], score_all.at[term], sc_ss.at[k - 1], sc_rs.at[k - 1],
            {"term": lax.rem(term + k, terms)},
        )

    def score_arrival(k):
        source = lax.rem(term + terms - k, terms)
        return remote(
            score_all.at[source], score_all.at[source], sc_ss.at[k - 1], sc_rs.at[k - 1],
            {"term": lax.rem(term + k, terms)},
        )

    def q_to_sibling(c):
        return remote(q_all.at[c, block], q_all.at[c, block], qs_ss.at[c], qs_rs.at[c], sibling)

    def q_from_sibling(c):
        at = chip * 2 + other
        return remote(q_all.at[c, at], q_all.at[c, at], qs_ss.at[c], qs_rs.at[c], sibling)

    def q_to_chip(c, k):
        return remote(
            q_all.at[c, block], q_all.at[c, block], qx_ss.at[c, k - 1], qx_rs.at[c, k - 1],
            {"batch": chip_up(k)},
        )

    def q_from_chip(c, k):
        at = chip_down(k) * 2 + core
        return remote(
            q_all.at[c, at], q_all.at[c, at], qx_ss.at[c, k - 1], qx_rs.at[c, k - 1],
            {"batch": chip_up(k)},
        )

    def q_forward(c, k):
        at = chip_down(k) * 2 + core
        return remote(
            q_all.at[c, at], q_all.at[c, at], qf_ss.at[c, k - 1], qf_rs.at[c, k - 1], sibling
        )

    def q_forwarded(c, k):
        at = chip_down(k) * 2 + other
        return remote(
            q_all.at[c, at], q_all.at[c, at], qf_ss.at[c, k - 1], qf_rs.at[c, k - 1], sibling
        )

    def p_copy(c):
        return remote(p_send.at[c], p_recv.at[c], p_ss.at[c], p_rs.at[c], sibling)

    def x_copy(c, k):
        return remote(
            x_send.at[c, k - 1], x_recv.at[c, k - 1], x_ss.at[c, k - 1], x_rs.at[c, k - 1],
            {"batch": chip_up(k)},
        )

    def s_copy(c):
        return remote(s_own.at[c], s_recv.at[c], s_ss.at[c], s_rs.at[c], sibling)

    def sx_copy(c, k):
        return remote(
            s_chip.at[c], s_far.at[c, k - 1], sx_ss.at[c, k - 1], sx_rs.at[c, k - 1],
            {"batch": chip_up(k)},
        )

    @pl.when(step == 0)
    def _():
        barrier = pltpu.get_barrier_semaphore()
        pl.semaphore_signal(barrier, inc=1, device_id=sibling, device_id_type=MESH)
        for k in range(1, chips):
            pl.semaphore_signal(barrier, inc=1, device_id={"batch": chip_up(k)}, device_id_type=MESH)
        for k in range(1, terms):
            pl.semaphore_signal(
                barrier, inc=1, device_id={"term": lax.rem(term + k, terms)}, device_id_type=MESH
            )
        pl.semaphore_wait(barrier, 1 + (chips - 1) + (terms - 1))
        score_all[term] = score_ref[...].astype(jnp.float32)
        for k in range(1, terms):
            score_copy(k).start()

    @pl.when(step < chunks)
    def _():
        c = step
        q_all[c, block] = impacts(q_in[...])
        for k in range(1, chips):
            q_to_chip(c, k).start()
        q_to_sibling(c).start()

    @pl.when(step == 0)
    def _():
        for k in range(1, terms):
            score_arrival(k).wait_recv()
        per = rows // score_all.shape[1]
        docs = score_all.shape[2]

        def score_block(at):
            return score_all[pl.ds(at * per, per)].reshape(rows, docs).astype(jnp.bfloat16)

        for k in range(chips):
            kept = chip_up(k) * 2
            score_keep_send[pl.ds(k * rows, rows), :] = score_block(kept + core)
            score_keep_send[pl.ds((chips + k) * rows, rows), :] = score_block(kept + other)
        ones = jnp.ones((16, docs), jnp.bfloat16)
        score_keep_send[pl.ds(2 * chips * rows, 16), :] = ones
        whole = score_all[...].reshape(2 * chips * rows, docs)
        score_t[pl.ds(0, docs), :] = whole.T.astype(jnp.bfloat16)
        score_t[pl.ds(docs, 16), :] = jnp.ones((16, 2 * chips * rows), jnp.bfloat16)
        for k in range(1, terms):
            score_copy(k).wait_send()

    @pl.when(step < chunks)
    def _():
        c = step
        half = chips * rows
        partial = jnp.dot(
            score_keep_send[...], impacts(d_in[...]), preferred_element_type=jnp.float32
        )
        width = partial.shape[1]
        p_send[c] = partial[half : 2 * half].astype(jnp.bfloat16).reshape(chips, rows, width)
        s_own[c] = partial[2 * half : 2 * half + 1]
        p_copy(c).start()
        s_copy(c).start()
        p_keep[c] = partial[:half].reshape(chips, rows, width)

    @pl.when(jnp.logical_and(step >= 1, step < chunks + 1))
    def _():
        c = step - 1
        p_copy(c).wait_recv()
        s_copy(c).wait_recv()
        for k in range(1, chips):
            x_send[c, k - 1] = (p_keep[c, k] + p_recv[c, k].astype(jnp.float32)).astype(jnp.bfloat16)
            x_copy(c, k).start()
        s_chip[c] = s_own[c] + s_recv[c]
        for k in range(1, chips):
            sx_copy(c, k).start()

    @pl.when(jnp.logical_and(step >= FORWARD_LAG, step < chunks + FORWARD_LAG))
    def _():
        c = step - FORWARD_LAG
        for k in range(1, chips):
            q_from_chip(c, k).wait_recv()
            q_forward(c, k).start()

    @pl.when(step >= OUT_LAG)
    def _():
        c = step - OUT_LAG
        q_from_sibling(c).wait_recv()
        for k in range(1, chips):
            q_forwarded(c, k).wait_recv()
        docs = d_in.shape[0]
        blocks = q_all.shape[1]
        width = q_all.shape[3]
        grads = jnp.dot(
            score_t[...], q_all[c].reshape(blocks * rows, width),
            preferred_element_type=jnp.float32,
        )
        for k in range(1, chips):
            x_copy(c, k).wait_recv()
            sx_copy(c, k).wait_recv()
        doc_sums = s_chip[c]
        for k in range(1, chips):
            doc_sums = doc_sums + s_far[c, k - 1]
        query_grad = p_keep[c, 0] + p_recv[c, 0].astype(jnp.float32)
        for k in range(1, chips):
            query_grad = query_grad + x_recv[c, k - 1].astype(jnp.float32)
        query_grad = query_grad + (2.0 * query_reg / num_queries) * grads[docs : docs + 1]
        q_out[...] = saturate_back(query_grad, q_again[...])
        doc_grad = grads[:docs] + (2.0 * doc_reg / num_docs) * doc_sums
        d_out[...] = saturate_back(doc_grad, d_again[...])
        q_to_sibling(c).wait_send()
        p_copy(c).wait_send()
        s_copy(c).wait_send()
        for k in range(1, chips):
            q_to_chip(c, k).wait_send()
            q_forward(c, k).wait_send()
            x_copy(c, k).wait_send()
            sx_copy(c, k).wait_send()


def on_device(chips, terms, query_logits, doc_logits, score_grad):
    rows, vocab = query_logits.shape
    docs = doc_logits.shape[0]
    score_rows = score_grad.shape[0]
    blocks = 2 * chips
    tiles = pl.cdiv(vocab, LANES)
    chunks = max(1, round(tiles / CHUNK_TILES))
    width = pl.cdiv(tiles, chunks) * LANES
    chunks = pl.cdiv(vocab, width)
    far = chips - 1

    def ahead(i):
        return 0, jnp.minimum(i, chunks - 1)

    def behind(i):
        return 0, jnp.maximum(i - OUT_LAG, 0)

    dma = pltpu.SemaphoreType.DMA
    scratch = [
        pltpu.VMEM((terms, score_rows, docs), jnp.float32),
        pltpu.VMEM((blocks * rows + 16, docs), jnp.bfloat16),
        pltpu.VMEM((docs + 16, blocks * rows), jnp.bfloat16),
        pltpu.VMEM((chunks, blocks, rows, width), jnp.bfloat16),
        pltpu.VMEM((chunks, chips, rows, width), jnp.float32),
        pltpu.VMEM((chunks, chips, rows, width), jnp.bfloat16),
        pltpu.VMEM((chunks, chips, rows, width), jnp.bfloat16),
        pltpu.VMEM((chunks, far, rows, width), jnp.bfloat16),
        pltpu.VMEM((chunks, far, rows, width), jnp.bfloat16),
        pltpu.VMEM((chunks, 1, width), jnp.float32),
        pltpu.VMEM((chunks, 1, width), jnp.float32),
        pltpu.VMEM((chunks, 1, width), jnp.float32),
        pltpu.VMEM((chunks, far, 1, width), jnp.float32),
        dma((terms - 1,)), dma((terms - 1,)),
        dma((chunks,)), dma((chunks,)),
        dma((chunks, far)), dma((chunks, far)),
        dma((chunks, far)), dma((chunks, far)),
        dma((chunks,)), dma((chunks,)),
        dma((chunks, far)), dma((chunks, far)),
        dma((chunks,)), dma((chunks,)),
        dma((chunks, far)), dma((chunks, far)),
    ]
    return pl.pallas_call(
        functools.partial(kernel, chips, terms, chunks, blocks * rows, blocks * docs),
        grid=(chunks + OUT_LAG,),
        out_shape=(
            jax.ShapeDtypeStruct(query_logits.shape, jnp.bfloat16),
            jax.ShapeDtypeStruct(doc_logits.shape, jnp.bfloat16),
        ),
        in_specs=[
            pl.BlockSpec((score_rows, docs), lambda i: (0, 0)),
            pl.BlockSpec((rows, width), ahead),
            pl.BlockSpec((docs, width), ahead),
            pl.BlockSpec((rows, width), behind),
            pl.BlockSpec((docs, width), behind),
        ],
        out_specs=(pl.BlockSpec((rows, width), behind), pl.BlockSpec((docs, width), behind)),
        scratch_shapes=scratch,
        compiler_params=pltpu.CompilerParams(
            collective_id=0,
            has_side_effects=True,
            vmem_limit_bytes=56 * 1024 * 1024,
            dimension_semantics=("arbitrary",),
        ),
        cost_estimate=pl.CostEstimate(
            flops=4 * docs * blocks * rows * vocab,
            bytes_accessed=6 * (rows + docs) * vocab,
            transcendentals=(rows + docs) * vocab,
        ),
    )(score_grad, query_logits, doc_logits, query_logits, doc_logits)


def solution(mesh):
    placed = (
        P(("grp", "batch", "sub"), "term"),
        P(("grp", "batch", "sub"), "term"),
        P(("grp", "term"), ("batch", "sub")),
    )
    return jax.shard_map(
        functools.partial(on_device, mesh.shape["batch"], mesh.shape["term"]),
        mesh=mesh,
        in_specs=placed,
        out_specs=(P(("grp", "batch", "sub"), "term"), P(("grp", "batch", "sub"), "term")),
        check_vma=False,
    )
```

```python
import functools

import jax
import jax.numpy as jnp
from jax import lax
from jax.experimental import pallas as pl
from jax.experimental.pallas import tpu as pltpu
from jax.sharding import PartitionSpec as P

query_reg = 1.0
doc_reg = 0.6

LANES = 128
CHUNK_TILES = 11
FORWARD_LAG = 2
OUT_LAG = 3
MESH = pl.DeviceIdType.MESH


def impacts(logits):
    return jnp.log1p(jnp.maximum(logits.astype(jnp.float32), 0.0)).astype(jnp.bfloat16)


def saturate_back(grad, logits):
    values = logits.astype(jnp.float32)
    scaled = grad / (1.0 + jnp.maximum(values, 0.0))
    return jnp.where(values > 0.0, scaled, 0.0).astype(jnp.bfloat16)


def kernel(
    chips, terms, chunks, num_queries, num_docs,
    score_ref, q_in, d_in, q_again, d_again, q_out, d_out,
    score_all, score_keep_send, score_rows,
    q_all, p_keep, p_send, p_recv, x_send, x_recv, s_own, s_recv, s_chip, s_far,
    sc_ss, sc_rs, qs_ss, qs_rs, qx_ss, qx_rs, qf_ss, qf_rs,
    p_ss, p_rs, x_ss, x_rs, s_ss, s_rs, sx_ss, sx_rs,
):
    step = pl.program_id(0)
    rows = q_in.shape[0]
    term = lax.axis_index("term")
    chip = lax.axis_index("batch")
    core = lax.axis_index("sub")
    other = 1 - core
    sibling = {"sub": other}
    block = chip * 2 + core

    def chip_up(k):
        return lax.rem(chip + k, chips)

    def chip_down(k):
        return lax.rem(chip + chips - k, chips)

    def remote(src, dst, send, recv, device):
        return pltpu.make_async_remote_copy(
            src_ref=src, dst_ref=dst, send_sem=send, recv_sem=recv,
            device_id=device, device_id_type=MESH,
        )

    def score_copy(k):
        return remote(
            score_all.at[term], score_all.at[term], sc_ss.at[k - 1], sc_rs.at[k - 1],
            {"term": lax.rem(term + k, terms)},
        )

    def score_arrival(k):
        source = lax.rem(term + terms - k, terms)
        return remote(
            score_all.at[source], score_all.at[source], sc_ss.at[k - 1], sc_rs.at[k - 1],
            {"term": lax.rem(term + k, terms)},
        )

    def q_to_sibling(c):
        return remote(q_all.at[c, block], q_all.at[c, block], qs_ss.at[c], qs_rs.at[c], sibling)

    def q_from_sibling(c):
        at = chip * 2 + other
        return remote(q_all.at[c, at], q_all.at[c, at], qs_ss.at[c], qs_rs.at[c], sibling)

    def q_to_chip(c, k):
        return remote(
            q_all.at[c, block], q_all.at[c, block], qx_ss.at[c, k - 1], qx_rs.at[c, k - 1],
            {"batch": chip_up(k)},
        )

    def q_from_chip(c, k):
        at = chip_down(k) * 2 + core
        return remote(
            q_all.at[c, at], q_all.at[c, at], qx_ss.at[c, k - 1], qx_rs.at[c, k - 1],
            {"batch": chip_up(k)},
        )

    def q_forward(c, k):
        at = chip_down(k) * 2 + core
        return remote(
            q_all.at[c, at], q_all.at[c, at], qf_ss.at[c, k - 1], qf_rs.at[c, k - 1], sibling
        )

    def q_forwarded(c, k):
        at = chip_down(k) * 2 + other
        return remote(
            q_all.at[c, at], q_all.at[c, at], qf_ss.at[c, k - 1], qf_rs.at[c, k - 1], sibling
        )

    def p_copy(c):
        return remote(p_send.at[c], p_recv.at[c], p_ss.at[c], p_rs.at[c], sibling)

    def x_copy(c, k):
        return remote(
            x_send.at[c, k - 1], x_recv.at[c, k - 1], x_ss.at[c, k - 1], x_rs.at[c, k - 1],
            {"batch": chip_up(k)},
        )

    def s_copy(c):
        return remote(s_own.at[c], s_recv.at[c], s_ss.at[c], s_rs.at[c], sibling)

    def sx_copy(c, k):
        return remote(
            s_chip.at[c], s_far.at[c, k - 1], sx_ss.at[c, k - 1], sx_rs.at[c, k - 1],
            {"batch": chip_up(k)},
        )

    @pl.when(step == 0)
    def _():
        barrier = pltpu.get_barrier_semaphore()
        pl.semaphore_signal(barrier, inc=1, device_id=sibling, device_id_type=MESH)
        for k in range(1, chips):
            pl.semaphore_signal(barrier, inc=1, device_id={"batch": chip_up(k)}, device_id_type=MESH)
        for k in range(1, terms):
            pl.semaphore_signal(
                barrier, inc=1, device_id={"term": lax.rem(term + k, terms)}, device_id_type=MESH
            )
        pl.semaphore_wait(barrier, 1 + (chips - 1) + (terms - 1))
        score_all[term] = score_ref[...].astype(jnp.float32)
        for k in range(1, terms):
            score_copy(k).start()

    @pl.when(step < chunks)
    def _():
        c = step
        q_all[c, block] = impacts(q_in[...])
        for k in range(1, chips):
            q_to_chip(c, k).start()
        q_to_sibling(c).start()

    @pl.when(step == 0)
    def _():
        for k in range(1, terms):
            score_arrival(k).wait_recv()
        per = rows // score_all.shape[1]
        docs = score_all.shape[2]

        def score_block(at):
            return score_all[pl.ds(at * per, per)].reshape(rows, docs).astype(jnp.bfloat16)

        for k in range(chips):
            kept = chip_up(k) * 2
            score_keep_send[pl.ds(k * rows, rows), :] = score_block(kept + core)
            score_keep_send[pl.ds((chips + k) * rows, rows), :] = score_block(kept + other)
        ones = jnp.ones((16, docs), jnp.bfloat16)
        score_keep_send[pl.ds(2 * chips * rows, 16), :] = ones
        whole = score_all[...].reshape(2 * chips * rows, docs)
        score_rows[pl.ds(0, 2 * chips * rows), :] = whole.astype(jnp.bfloat16)
        score_rows[pl.ds(2 * chips * rows, 16), :] = ones
        for k in range(1, terms):
            score_copy(k).wait_send()

    @pl.when(step < chunks)
    def _():
        c = step
        half = chips * rows
        partial = lax.dot_general(
            score_keep_send[...], impacts(d_in[...]), (((1,), (1,)), ((), ())),
            preferred_element_type=jnp.float32,
        )
        width = partial.shape[1]
        p_send[c] = partial[half : 2 * half].astype(jnp.bfloat16).reshape(chips, rows, width)
        s_own[c] = partial[2 * half : 2 * half + 1]
        p_copy(c).start()
        s_copy(c).start()
        p_keep[c] = partial[:half].reshape(chips, rows, width)

    @pl.when(jnp.logical_and(step >= 1, step < chunks + 1))
    def _():
        c = step - 1
        p_copy(c).wait_recv()
        s_copy(c).wait_recv()
        for k in range(1, chips):
            x_send[c, k - 1] = (p_keep[c, k] + p_recv[c, k].astype(jnp.float32)).astype(jnp.bfloat16)
            x_copy(c, k).start()
        s_chip[c] = s_own[c] + s_recv[c]
        for k in range(1, chips):
            sx_copy(c, k).start()

    @pl.when(jnp.logical_and(step >= FORWARD_LAG, step < chunks + FORWARD_LAG))
    def _():
        c = step - FORWARD_LAG
        for k in range(1, chips):
            q_from_chip(c, k).wait_recv()
            q_forward(c, k).start()

    @pl.when(step >= OUT_LAG)
    def _():
        c = step - OUT_LAG
        q_from_sibling(c).wait_recv()
        for k in range(1, chips):
            q_forwarded(c, k).wait_recv()
        blocks = q_all.shape[1]
        width = q_all.shape[3]
        all_impacts = q_all[c].reshape(blocks * rows, width)
        query_sums = jnp.dot(
            jnp.ones((16, blocks * rows), jnp.bfloat16), all_impacts,
            preferred_element_type=jnp.float32,
        )[:1]
        for k in range(1, chips):
            x_copy(c, k).wait_recv()
            sx_copy(c, k).wait_recv()
        doc_sums = s_chip[c]
        for k in range(1, chips):
            doc_sums = doc_sums + s_far[c, k - 1]
        query_grad = p_keep[c, 0] + p_recv[c, 0].astype(jnp.float32)
        for k in range(1, chips):
            query_grad = query_grad + x_recv[c, k - 1].astype(jnp.float32)
        query_grad = query_grad + (2.0 * query_reg / num_queries) * query_sums
        q_out[...] = saturate_back(query_grad, q_again[...])
        doc_reg_grad = (2.0 * doc_reg / num_docs) * doc_sums
        high = doc_reg_grad.astype(jnp.bfloat16)
        left = doc_reg_grad - high.astype(jnp.float32)
        middle = left.astype(jnp.bfloat16)
        low = (left - middle.astype(jnp.float32)).astype(jnp.bfloat16)
        parts = jnp.concatenate(
            [high, middle, low, jnp.zeros((13, width), jnp.bfloat16)], axis=0
        )
        doc_grad = lax.dot_general(
            jnp.concatenate([all_impacts, parts], axis=0), score_rows[...],
            (((0,), (0,)), ((), ())), preferred_element_type=jnp.float32,
        )
        d_out[...] = saturate_back(doc_grad, d_again[...])
        q_to_sibling(c).wait_send()
        p_copy(c).wait_send()
        s_copy(c).wait_send()
        for k in range(1, chips):
            q_to_chip(c, k).wait_send()
            q_forward(c, k).wait_send()
            x_copy(c, k).wait_send()
            sx_copy(c, k).wait_send()


def on_device(chips, terms, query_logits, doc_logits, score_grad):
    rows, vocab = query_logits.shape
    docs = doc_logits.shape[0]
    doc_logits = doc_logits.T
    score_rows = score_grad.shape[0]
    blocks = 2 * chips
    tiles = pl.cdiv(vocab, LANES)
    chunks = max(1, round(tiles / CHUNK_TILES))
    width = pl.cdiv(tiles, chunks) * LANES
    chunks = pl.cdiv(vocab, width)
    far = chips - 1

    def ahead(i):
        return 0, jnp.minimum(i, chunks - 1)

    def behind(i):
        return 0, jnp.maximum(i - OUT_LAG, 0)

    def ahead_docs(i):
        return jnp.minimum(i, chunks - 1), 0

    def behind_docs(i):
        return jnp.maximum(i - OUT_LAG, 0), 0

    dma = pltpu.SemaphoreType.DMA
    scratch = [
        pltpu.VMEM((terms, score_rows, docs), jnp.float32),
        pltpu.VMEM((blocks * rows + 16, docs), jnp.bfloat16),
        pltpu.VMEM((blocks * rows + 16, docs), jnp.bfloat16),
        pltpu.VMEM((chunks, blocks, rows, width), jnp.bfloat16),
        pltpu.VMEM((chunks, chips, rows, width), jnp.float32),
        pltpu.VMEM((chunks, chips, rows, width), jnp.bfloat16),
        pltpu.VMEM((chunks, chips, rows, width), jnp.bfloat16),
        pltpu.VMEM((chunks, far, rows, width), jnp.bfloat16),
        pltpu.VMEM((chunks, far, rows, width), jnp.bfloat16),
        pltpu.VMEM((chunks, 1, width), jnp.float32),
        pltpu.VMEM((chunks, 1, width), jnp.float32),
        pltpu.VMEM((chunks, 1, width), jnp.float32),
        pltpu.VMEM((chunks, far, 1, width), jnp.float32),
        dma((terms - 1,)), dma((terms - 1,)),
        dma((chunks,)), dma((chunks,)),
        dma((chunks, far)), dma((chunks, far)),
        dma((chunks, far)), dma((chunks, far)),
        dma((chunks,)), dma((chunks,)),
        dma((chunks, far)), dma((chunks, far)),
        dma((chunks,)), dma((chunks,)),
        dma((chunks, far)), dma((chunks, far)),
    ]
    query_grad, doc_grad = pl.pallas_call(
        functools.partial(kernel, chips, terms, chunks, blocks * rows, blocks * docs),
        grid=(chunks + OUT_LAG,),
        out_shape=(
            jax.ShapeDtypeStruct(query_logits.shape, jnp.bfloat16),
            jax.ShapeDtypeStruct(doc_logits.shape, jnp.bfloat16),
        ),
        in_specs=[
            pl.BlockSpec((score_rows, docs), lambda i: (0, 0)),
            pl.BlockSpec((rows, width), ahead),
            pl.BlockSpec((width, docs), ahead_docs),
            pl.BlockSpec((rows, width), behind),
            pl.BlockSpec((width, docs), behind_docs),
        ],
        out_specs=(pl.BlockSpec((rows, width), behind), pl.BlockSpec((width, docs), behind_docs)),
        scratch_shapes=scratch,
        compiler_params=pltpu.CompilerParams(
            collective_id=0,
            has_side_effects=True,
            vmem_limit_bytes=56 * 1024 * 1024,
            dimension_semantics=("arbitrary",),
        ),
        cost_estimate=pl.CostEstimate(
            flops=4 * docs * blocks * rows * vocab,
            bytes_accessed=6 * (rows + docs) * vocab,
            transcendentals=(rows + docs) * vocab,
        ),
    )(score_grad, query_logits, doc_logits, query_logits, doc_logits)
    return query_grad, doc_grad.T


def solution(mesh):
    placed = (
        P(("grp", "batch", "sub"), "term"),
        P(("grp", "batch", "sub"), "term"),
        P(("grp", "term"), ("batch", "sub")),
    )
    return jax.shard_map(
        functools.partial(on_device, mesh.shape["batch"], mesh.shape["term"]),
        mesh=mesh,
        in_specs=placed,
        out_specs=(P(("grp", "batch", "sub"), "term"), P(("grp", "batch", "sub"), "term")),
        check_vma=False,
    )
```

```python
import functools

import jax
import jax.numpy as jnp
from jax import lax
from jax.experimental import pallas as pl
from jax.experimental.pallas import tpu as pltpu
from jax.sharding import PartitionSpec as P

query_reg = 1.0
doc_reg = 0.6

LANES = 128
CHUNK_TILES = 11
FORWARD_LAG = 2
OUT_LAG = 3
MESH = pl.DeviceIdType.MESH


def impacts(logits):
    return jnp.log1p(jnp.maximum(logits.astype(jnp.float32), 0.0)).astype(jnp.bfloat16)


def saturate_back(grad, logits):
    values = logits.astype(jnp.float32)
    scaled = grad / (1.0 + jnp.maximum(values, 0.0))
    return jnp.where(values > 0.0, scaled, 0.0).astype(jnp.bfloat16)


def kernel(
    chips, terms, chunks, num_queries, num_docs,
    score_ref, q_in, d_in, q_again, d_again, q_out, d_out,
    score_all, score_keep_send, score_rows,
    q_all, p_keep, p_send, p_recv, x_send, x_recv, s_own, s_recv, s_chip, s_far,
    sc_ss, sc_rs, qs_ss, qs_rs, qx_ss, qx_rs, qf_ss, qf_rs,
    p_ss, p_rs, x_ss, x_rs, s_ss, s_rs, sx_ss, sx_rs,
    q_ring, d_ring, qw_sem, dw_sem,
):
    step = pl.program_id(0)
    rows = q_in.shape[0]
    term = lax.axis_index("term")
    chip = lax.axis_index("batch")
    core = lax.axis_index("sub")
    other = 1 - core
    sibling = {"sub": other}
    block = chip * 2 + core

    def chip_up(k):
        return lax.rem(chip + k, chips)

    def chip_down(k):
        return lax.rem(chip + chips - k, chips)

    def remote(src, dst, send, recv, device):
        return pltpu.make_async_remote_copy(
            src_ref=src, dst_ref=dst, send_sem=send, recv_sem=recv,
            device_id=device, device_id_type=MESH,
        )

    def score_copy(k):
        return remote(
            score_all.at[term], score_all.at[term], sc_ss.at[k - 1], sc_rs.at[k - 1],
            {"term": lax.rem(term + k, terms)},
        )

    def score_arrival(k):
        source = lax.rem(term + terms - k, terms)
        return remote(
            score_all.at[source], score_all.at[source], sc_ss.at[k - 1], sc_rs.at[k - 1],
            {"term": lax.rem(term + k, terms)},
        )

    def q_to_sibling(c):
        return remote(q_all.at[c, block], q_all.at[c, block], qs_ss.at[c], qs_rs.at[c], sibling)

    def q_from_sibling(c):
        at = chip * 2 + other
        return remote(q_all.at[c, at], q_all.at[c, at], qs_ss.at[c], qs_rs.at[c], sibling)

    def q_to_chip(c, k):
        return remote(
            q_all.at[c, block], q_all.at[c, block], qx_ss.at[c, k - 1], qx_rs.at[c, k - 1],
            {"batch": chip_up(k)},
        )

    def q_from_chip(c, k):
        at = chip_down(k) * 2 + core
        return remote(
            q_all.at[c, at], q_all.at[c, at], qx_ss.at[c, k - 1], qx_rs.at[c, k - 1],
            {"batch": chip_up(k)},
        )

    def q_forward(c, k):
        at = chip_down(k) * 2 + core
        return remote(
            q_all.at[c, at], q_all.at[c, at], qf_ss.at[c, k - 1], qf_rs.at[c, k - 1], sibling
        )

    def q_forwarded(c, k):
        at = chip_down(k) * 2 + other
        return remote(
            q_all.at[c, at], q_all.at[c, at], qf_ss.at[c, k - 1], qf_rs.at[c, k - 1], sibling
        )

    def p_copy(c):
        return remote(p_send.at[c], p_recv.at[c], p_ss.at[c], p_rs.at[c], sibling)

    def x_copy(c, k):
        return remote(
            x_send.at[c, k - 1], x_recv.at[c, k - 1], x_ss.at[c, k - 1], x_rs.at[c, k - 1],
            {"batch": chip_up(k)},
        )

    def s_copy(c):
        return remote(s_own.at[c], s_recv.at[c], s_ss.at[c], s_rs.at[c], sibling)

    def sx_copy(c, k):
        return remote(
            s_chip.at[c], s_far.at[c, k - 1], sx_ss.at[c, k - 1], sx_rs.at[c, k - 1],
            {"batch": chip_up(k)},
        )

    width = q_in.shape[1]

    def q_write(c):
        slot = lax.rem(c, 2)
        return pltpu.make_async_copy(q_ring.at[slot], q_out.at[c], qw_sem.at[slot])

    def d_write(c):
        slot = lax.rem(c, 2)
        return pltpu.make_async_copy(
            d_ring.at[slot], d_out.at[pl.ds(pl.multiple_of(c * width, LANES), width)], dw_sem.at[slot]
        )

    @pl.when(step == 0)
    def _():
        barrier = pltpu.get_barrier_semaphore()
        pl.semaphore_signal(barrier, inc=1, device_id=sibling, device_id_type=MESH)
        for k in range(1, chips):
            pl.semaphore_signal(barrier, inc=1, device_id={"batch": chip_up(k)}, device_id_type=MESH)
        for k in range(1, terms):
            pl.semaphore_signal(
                barrier, inc=1, device_id={"term": lax.rem(term + k, terms)}, device_id_type=MESH
            )
        pl.semaphore_wait(barrier, 1 + (chips - 1) + (terms - 1))
        score_all[term] = score_ref[...].astype(jnp.float32)
        for k in range(1, terms):
            score_copy(k).start()

    @pl.when(step < chunks)
    def _():
        c = step
        q_all[c, block] = impacts(q_in[...])
        for k in range(1, chips):
            q_to_chip(c, k).start()
        q_to_sibling(c).start()

    @pl.when(step == 0)
    def _():
        for k in range(1, terms):
            score_arrival(k).wait_recv()
        per = rows // score_all.shape[1]
        docs = score_all.shape[2]

        def score_block(at):
            return score_all[pl.ds(at * per, per)].reshape(rows, docs).astype(jnp.bfloat16)

        for k in range(chips):
            kept = chip_up(k) * 2
            score_keep_send[pl.ds(k * rows, rows), :] = score_block(kept + core)
            score_keep_send[pl.ds((chips + k) * rows, rows), :] = score_block(kept + other)
        ones = jnp.ones((16, docs), jnp.bfloat16)
        score_keep_send[pl.ds(2 * chips * rows, 16), :] = ones
        whole = score_all[...].reshape(2 * chips * rows, docs)
        score_rows[pl.ds(0, 2 * chips * rows), :] = whole.astype(jnp.bfloat16)
        score_rows[pl.ds(2 * chips * rows, 16), :] = ones
        for k in range(1, terms):
            score_copy(k).wait_send()

    @pl.when(step < chunks)
    def _():
        c = step
        half = chips * rows
        partial = lax.dot_general(
            score_keep_send[...], impacts(d_in[...]), (((1,), (1,)), ((), ())),
            preferred_element_type=jnp.float32,
        )
        width = partial.shape[1]
        p_send[c] = partial[half : 2 * half].astype(jnp.bfloat16).reshape(chips, rows, width)
        s_own[c] = partial[2 * half : 2 * half + 1]
        p_copy(c).start()
        s_copy(c).start()
        p_keep[c] = partial[:half].reshape(chips, rows, width)

    @pl.when(jnp.logical_and(step >= 1, step < chunks + 1))
    def _():
        c = step - 1
        p_copy(c).wait_recv()
        s_copy(c).wait_recv()
        for k in range(1, chips):
            x_send[c, k - 1] = (p_keep[c, k] + p_recv[c, k].astype(jnp.float32)).astype(jnp.bfloat16)
            x_copy(c, k).start()
        s_chip[c] = s_own[c] + s_recv[c]
        for k in range(1, chips):
            sx_copy(c, k).start()

    @pl.when(jnp.logical_and(step >= FORWARD_LAG, step < chunks + FORWARD_LAG))
    def _():
        c = step - FORWARD_LAG
        for k in range(1, chips):
            q_from_chip(c, k).wait_recv()
            q_forward(c, k).start()

    @pl.when(step >= OUT_LAG)
    def _():
        c = step - OUT_LAG
        q_from_sibling(c).wait_recv()
        for k in range(1, chips):
            q_forwarded(c, k).wait_recv()
        blocks = q_all.shape[1]
        width = q_all.shape[3]
        all_impacts = q_all[c].reshape(blocks * rows, width)
        query_sums = jnp.dot(
            jnp.ones((16, blocks * rows), jnp.bfloat16), all_impacts,
            preferred_element_type=jnp.float32,
        )[:1]
        for k in range(1, chips):
            x_copy(c, k).wait_recv()
            sx_copy(c, k).wait_recv()
        doc_sums = s_chip[c]
        for k in range(1, chips):
            doc_sums = doc_sums + s_far[c, k - 1]
        query_grad = p_keep[c, 0] + p_recv[c, 0].astype(jnp.float32)
        for k in range(1, chips):
            query_grad = query_grad + x_recv[c, k - 1].astype(jnp.float32)
        query_grad = query_grad + (2.0 * query_reg / num_queries) * query_sums
        slot = lax.rem(c, 2)

        @pl.when(c >= 2)
        def _():
            q_write(c - 2).wait()
            d_write(c - 2).wait()

        q_ring[slot] = saturate_back(query_grad, q_again[...])
        doc_reg_grad = (2.0 * doc_reg / num_docs) * doc_sums
        high = doc_reg_grad.astype(jnp.bfloat16)
        left = doc_reg_grad - high.astype(jnp.float32)
        middle = left.astype(jnp.bfloat16)
        low = (left - middle.astype(jnp.float32)).astype(jnp.bfloat16)
        parts = jnp.concatenate(
            [high, middle, low, jnp.zeros((13, width), jnp.bfloat16)], axis=0
        )
        doc_grad = lax.dot_general(
            jnp.concatenate([all_impacts, parts], axis=0), score_rows[...],
            (((0,), (0,)), ((), ())), preferred_element_type=jnp.float32,
        )
        d_ring[slot] = saturate_back(doc_grad, d_again[...])
        q_write(c).start()
        d_write(c).start()
        q_to_sibling(c).wait_send()
        p_copy(c).wait_send()
        s_copy(c).wait_send()
        for k in range(1, chips):
            q_to_chip(c, k).wait_send()
            q_forward(c, k).wait_send()
            x_copy(c, k).wait_send()
            sx_copy(c, k).wait_send()

        @pl.when(c == chunks - 1)
        def _():
            for last in range(max(0, chunks - 2), chunks):
                q_write(last).wait()
                d_write(last).wait()


def on_device(chips, terms, query_logits, doc_logits, score_grad):
    rows, vocab = query_logits.shape
    docs = doc_logits.shape[0]
    doc_logits = doc_logits.T
    score_rows = score_grad.shape[0]
    blocks = 2 * chips
    tiles = pl.cdiv(vocab, LANES)
    chunks = max(1, round(tiles / CHUNK_TILES))
    width = pl.cdiv(tiles, chunks) * LANES
    chunks = pl.cdiv(vocab, width)
    far = chips - 1

    def ahead(i):
        return 0, jnp.minimum(i, chunks - 1)

    def behind(i):
        return 0, jnp.maximum(i - OUT_LAG, 0)

    def ahead_docs(i):
        return jnp.minimum(i, chunks - 1), 0

    def behind_docs(i):
        return jnp.maximum(i - OUT_LAG, 0), 0

    dma = pltpu.SemaphoreType.DMA
    scratch = [
        pltpu.VMEM((terms, score_rows, docs), jnp.float32),
        pltpu.VMEM((blocks * rows + 16, docs), jnp.bfloat16),
        pltpu.VMEM((blocks * rows + 16, docs), jnp.bfloat16),
        pltpu.VMEM((chunks, blocks, rows, width), jnp.bfloat16),
        pltpu.VMEM((chunks, chips, rows, width), jnp.float32),
        pltpu.VMEM((chunks, chips, rows, width), jnp.bfloat16),
        pltpu.VMEM((chunks, chips, rows, width), jnp.bfloat16),
        pltpu.VMEM((chunks, far, rows, width), jnp.bfloat16),
        pltpu.VMEM((chunks, far, rows, width), jnp.bfloat16),
        pltpu.VMEM((chunks, 1, width), jnp.float32),
        pltpu.VMEM((chunks, 1, width), jnp.float32),
        pltpu.VMEM((chunks, 1, width), jnp.float32),
        pltpu.VMEM((chunks, far, 1, width), jnp.float32),
        dma((terms - 1,)), dma((terms - 1,)),
        dma((chunks,)), dma((chunks,)),
        dma((chunks, far)), dma((chunks, far)),
        dma((chunks, far)), dma((chunks, far)),
        dma((chunks,)), dma((chunks,)),
        dma((chunks, far)), dma((chunks, far)),
        dma((chunks,)), dma((chunks,)),
        dma((chunks, far)), dma((chunks, far)),
        pltpu.VMEM((2, rows, width), jnp.bfloat16),
        pltpu.VMEM((2, width, docs), jnp.bfloat16),
        dma((2,)), dma((2,)),
    ]
    query_grad, doc_grad = pl.pallas_call(
        functools.partial(kernel, chips, terms, chunks, blocks * rows, blocks * docs),
        grid=(chunks + OUT_LAG,),
        out_shape=(
            pltpu.VMEM((chunks, rows, width), jnp.bfloat16),
            pltpu.VMEM((chunks * width, docs), jnp.bfloat16),
        ),
        in_specs=[
            pl.BlockSpec((score_rows, docs), lambda i: (0, 0)),
            pl.BlockSpec((rows, width), ahead),
            pl.BlockSpec((width, docs), ahead_docs),
            pl.BlockSpec((rows, width), behind),
            pl.BlockSpec((width, docs), behind_docs),
        ],
        out_specs=(pl.BlockSpec(memory_space=pl.ANY), pl.BlockSpec(memory_space=pl.ANY)),
        scratch_shapes=scratch,
        compiler_params=pltpu.CompilerParams(
            collective_id=0,
            has_side_effects=True,
            vmem_limit_bytes=46 * 1024 * 1024,
            dimension_semantics=("arbitrary",),
        ),
        cost_estimate=pl.CostEstimate(
            flops=4 * docs * blocks * rows * vocab,
            bytes_accessed=6 * (rows + docs) * vocab,
            transcendentals=(rows + docs) * vocab,
        ),
    )(score_grad, query_logits, doc_logits, query_logits, doc_logits)
    query_grad = query_grad.transpose(1, 0, 2).reshape(rows, chunks * width)[:, :vocab]
    return query_grad, doc_grad[:vocab].T


def solution(mesh):
    placed = (
        P(("grp", "batch", "sub"), "term"),
        P(("grp", "batch", "sub"), "term"),
        P(("grp", "term"), ("batch", "sub")),
    )
    return jax.shard_map(
        functools.partial(on_device, mesh.shape["batch"], mesh.shape["term"]),
        mesh=mesh,
        in_specs=placed,
        out_specs=(P(("grp", "batch", "sub"), "term"), P(("grp", "batch", "sub"), "term")),
        check_vma=False,
    )
```

```python
import functools

import jax
import jax.numpy as jnp
from jax import lax
from jax.experimental import pallas as pl
from jax.experimental.pallas import tpu as pltpu
from jax.sharding import PartitionSpec as P

query_reg = 1.0
doc_reg = 0.6

LANES = 128
CHUNK_TILES = 27
FORWARD_LAG = 2
OUT_LAG = 3
MESH = pl.DeviceIdType.MESH


def impacts(logits):
    return jnp.log1p(jnp.maximum(logits.astype(jnp.float32), 0.0)).astype(jnp.bfloat16)


def saturate_back(grad, logits):
    values = logits.astype(jnp.float32)
    scaled = grad / (1.0 + jnp.maximum(values, 0.0))
    return jnp.where(values > 0.0, scaled, 0.0).astype(jnp.bfloat16)


def kernel(
    chips, terms, chunks, num_queries, num_docs,
    score_ref, q_in, d_in, q_again, d_again, q_out, d_out,
    score_all, score_keep_send, score_rows,
    q_all, p_keep, p_send, p_recv, x_send, x_recv, s_own, s_recv, s_chip, s_pack, s_far, s_rows,
    sc_ss, sc_rs, qs_ss, qs_rs, qx_ss, qx_rs, qf_ss, qf_rs,
    p_ss, p_rs, x_ss, x_rs, s_ss, s_rs, sx_ss, sx_rs, sf_ss, sf_rs,
    q_ring, d_ring, qw_sem, dw_sem,
):
    step = pl.program_id(0)
    rows = q_in.shape[0]
    term = lax.axis_index("term")
    chip = lax.axis_index("batch")
    core = lax.axis_index("sub")
    other = 1 - core
    sibling = {"sub": other}
    block = chip * 2 + core

    def chip_up(k):
        return lax.rem(chip + k, chips)

    def chip_down(k):
        return lax.rem(chip + chips - k, chips)

    def remote(src, dst, send, recv, device):
        return pltpu.make_async_remote_copy(
            src_ref=src, dst_ref=dst, send_sem=send, recv_sem=recv,
            device_id=device, device_id_type=MESH,
        )

    def score_copy(k):
        return remote(
            score_all.at[term], score_all.at[term], sc_ss.at[k - 1], sc_rs.at[k - 1],
            {"term": lax.rem(term + k, terms)},
        )

    def score_arrival(k):
        source = lax.rem(term + terms - k, terms)
        return remote(
            score_all.at[source], score_all.at[source], sc_ss.at[k - 1], sc_rs.at[k - 1],
            {"term": lax.rem(term + k, terms)},
        )

    def q_to_sibling(c):
        return remote(q_all.at[c, block], q_all.at[c, block], qs_ss.at[c], qs_rs.at[c], sibling)

    def q_from_sibling(c):
        at = chip * 2 + other
        return remote(q_all.at[c, at], q_all.at[c, at], qs_ss.at[c], qs_rs.at[c], sibling)

    def q_to_chip(c, k):
        return remote(
            q_all.at[c, block], q_all.at[c, block], qx_ss.at[c, k - 1], qx_rs.at[c, k - 1],
            {"batch": chip_up(k)},
        )

    def q_from_chip(c, k):
        at = chip_down(k) * 2 + core
        return remote(
            q_all.at[c, at], q_all.at[c, at], qx_ss.at[c, k - 1], qx_rs.at[c, k - 1],
            {"batch": chip_up(k)},
        )

    def q_forward(c, k):
        at = chip_down(k) * 2 + core
        return remote(
            q_all.at[c, at], q_all.at[c, at], qf_ss.at[c, k - 1], qf_rs.at[c, k - 1], sibling
        )

    def q_forwarded(c, k):
        at = chip_down(k) * 2 + other
        return remote(
            q_all.at[c, at], q_all.at[c, at], qf_ss.at[c, k - 1], qf_rs.at[c, k - 1], sibling
        )

    def p_copy(c):
        return remote(p_send.at[c], p_recv.at[c], p_ss.at[c], p_rs.at[c], sibling)

    def x_copy(c, k):
        return remote(
            x_send.at[c, k - 1], x_recv.at[c, k - 1], x_ss.at[c, k - 1], x_rs.at[c, k - 1],
            {"batch": chip_up(k)},
        )

    def s_copy(c):
        return remote(s_own.at[c], s_recv.at[c], s_ss.at[c], s_rs.at[c], sibling)

    def sx_copy(c, k):
        return remote(
            s_pack.at[c, core], s_far.at[c, k - 1, core], sx_ss.at[c, k - 1], sx_rs.at[c, k - 1],
            {"batch": chip_up(k)},
        )

    def s_forward(c, k):
        return remote(
            s_far.at[c, k - 1, core], s_far.at[c, k - 1, core],
            sf_ss.at[c, k - 1], sf_rs.at[c, k - 1], sibling,
        )

    def s_forwarded(c, k):
        return remote(
            s_far.at[c, k - 1, other], s_far.at[c, k - 1, other],
            sf_ss.at[c, k - 1], sf_rs.at[c, k - 1], sibling,
        )

    width = q_in.shape[1]
    tiles = width // LANES
    half_tiles = pl.cdiv(tiles, 2)

    def q_write(c):
        slot = lax.rem(c, 2)
        return pltpu.make_async_copy(q_ring.at[slot], q_out.at[c], qw_sem.at[slot])

    def d_write(c):
        slot = lax.rem(c, 2)
        return pltpu.make_async_copy(
            d_ring.at[slot], d_out.at[pl.ds(pl.multiple_of(c * width, LANES), width)], dw_sem.at[slot]
        )

    @pl.when(step == 0)
    def _():
        barrier = pltpu.get_barrier_semaphore()
        pl.semaphore_signal(barrier, inc=1, device_id=sibling, device_id_type=MESH)
        for k in range(1, chips):
            pl.semaphore_signal(barrier, inc=1, device_id={"batch": chip_up(k)}, device_id_type=MESH)
        for k in range(1, terms):
            pl.semaphore_signal(
                barrier, inc=1, device_id={"term": lax.rem(term + k, terms)}, device_id_type=MESH
            )
        pl.semaphore_wait(barrier, 1 + (chips - 1) + (terms - 1))
        s_rows[...] = jnp.zeros_like(s_rows)
        score_all[term] = score_ref[...].astype(jnp.float32)
        for k in range(1, terms):
            score_copy(k).start()

    @pl.when(step < chunks)
    def _():
        c = step
        q_all[c, block] = impacts(q_in[...])
        for k in range(1, chips):
            q_to_chip(c, k).start()
        q_to_sibling(c).start()

    @pl.when(step == 0)
    def _():
        for k in range(1, terms):
            score_arrival(k).wait_recv()
        per = rows // score_all.shape[1]
        docs = score_all.shape[2]

        def score_block(at):
            return score_all[pl.ds(at * per, per)].reshape(rows, docs).astype(jnp.bfloat16)

        for k in range(chips):
            kept = chip_up(k) * 2
            score_keep_send[pl.ds(k * rows, rows), :] = score_block(kept + core)
            score_keep_send[pl.ds((chips + k) * rows, rows), :] = score_block(kept + other)
        ones = jnp.ones((16, docs), jnp.bfloat16)
        score_keep_send[pl.ds(2 * chips * rows, 16), :] = ones
        whole = score_all[...].reshape(2 * chips * rows, docs)
        score_rows[pl.ds(0, 2 * chips * rows), :] = whole.astype(jnp.bfloat16)
        score_rows[pl.ds(2 * chips * rows, 16), :] = ones
        for k in range(1, terms):
            score_copy(k).wait_send()

    @pl.when(step < chunks)
    def _():
        c = step
        half = chips * rows
        partial = lax.dot_general(
            score_keep_send[...], impacts(d_in[...]), (((1,), (1,)), ((), ())),
            preferred_element_type=jnp.float32,
        )
        width = partial.shape[1]
        p_send[c] = partial[half : 2 * half].astype(jnp.bfloat16).reshape(chips, rows, width)
        s_own[c] = partial[2 * half : 2 * half + 1]
        p_copy(c).start()
        s_copy(c).start()
        p_keep[c] = partial[:half].reshape(chips, rows, width)

    @pl.when(jnp.logical_and(step >= 1, step < chunks + 1))
    def _():
        c = step - 1
        p_copy(c).wait_recv()
        s_copy(c).wait_recv()
        chip_sums = s_own[c] + s_recv[c]
        s_chip[c] = chip_sums
        for t in range(tiles):
            h, r = divmod(t, half_tiles)
            s_rows[h, r : r + 1, :] = chip_sums[:, t * LANES : (t + 1) * LANES]
        s_pack[c] = s_rows[...].astype(jnp.bfloat16)
        for k in range(1, chips):
            sx_copy(c, k).start()
        for k in range(1, chips):
            x_send[c, k - 1] = (p_keep[c, k] + p_recv[c, k].astype(jnp.float32)).astype(jnp.bfloat16)
            x_copy(c, k).start()

    @pl.when(jnp.logical_and(step >= FORWARD_LAG, step < chunks + FORWARD_LAG))
    def _():
        c = step - FORWARD_LAG
        for k in range(1, chips):
            q_from_chip(c, k).wait_recv()
            q_forward(c, k).start()
            sx_copy(c, k).wait_recv()
            s_forward(c, k).start()

    @pl.when(step >= OUT_LAG)
    def _():
        c = step - OUT_LAG
        q_from_sibling(c).wait_recv()
        for k in range(1, chips):
            q_forwarded(c, k).wait_recv()
        blocks = q_all.shape[1]
        width = q_all.shape[3]
        all_impacts = q_all[c].reshape(blocks * rows, width)
        query_sums = jnp.dot(
            jnp.ones((16, blocks * rows), jnp.bfloat16), all_impacts,
            preferred_element_type=jnp.float32,
        )[:1]
        doc_sums = s_chip[c]
        for k in range(1, chips):
            s_forwarded(c, k).wait_recv()
            s_rows[...] = s_far[c, k - 1].astype(jnp.float32)
            pieces = []
            for t in range(tiles):
                h, r = divmod(t, half_tiles)
                pieces.append(s_rows[h, r : r + 1, :])
            doc_sums = doc_sums + jnp.concatenate(pieces, axis=1)
        slot = lax.rem(c, 2)

        @pl.when(c >= 2)
        def _():
            q_write(c - 2).wait()
            d_write(c - 2).wait()

        doc_reg_grad = (2.0 * doc_reg / num_docs) * doc_sums
        high = doc_reg_grad.astype(jnp.bfloat16)
        left = doc_reg_grad - high.astype(jnp.float32)
        middle = left.astype(jnp.bfloat16)
        low = (left - middle.astype(jnp.float32)).astype(jnp.bfloat16)
        parts = jnp.concatenate(
            [high, middle, low, jnp.zeros((13, width), jnp.bfloat16)], axis=0
        )
        doc_grad = lax.dot_general(
            jnp.concatenate([all_impacts, parts], axis=0), score_rows[...],
            (((0,), (0,)), ((), ())), preferred_element_type=jnp.float32,
        )
        d_ring[slot] = saturate_back(doc_grad, d_again[...])
        d_write(c).start()
        query_grad = p_keep[c, 0] + p_recv[c, 0].astype(jnp.float32)
        query_grad = query_grad + (2.0 * query_reg / num_queries) * query_sums
        for k in range(1, chips):
            x_copy(c, k).wait_recv()
            query_grad = query_grad + x_recv[c, k - 1].astype(jnp.float32)
        q_ring[slot] = saturate_back(query_grad, q_again[...])
        q_write(c).start()
        q_to_sibling(c).wait_send()
        p_copy(c).wait_send()
        s_copy(c).wait_send()
        for k in range(1, chips):
            q_to_chip(c, k).wait_send()
            q_forward(c, k).wait_send()
            x_copy(c, k).wait_send()
            sx_copy(c, k).wait_send()
            s_forward(c, k).wait_send()

        @pl.when(c == chunks - 1)
        def _():
            for last in range(max(0, chunks - 2), chunks):
                q_write(last).wait()
                d_write(last).wait()


def on_device(chips, terms, query_logits, doc_logits, score_grad):
    rows, vocab = query_logits.shape
    docs = doc_logits.shape[0]
    doc_logits = doc_logits.T
    score_rows = score_grad.shape[0]
    blocks = 2 * chips
    tiles = pl.cdiv(vocab, LANES)
    chunks = max(1, round(tiles / CHUNK_TILES))
    width = pl.cdiv(tiles, chunks) * LANES
    chunks = pl.cdiv(vocab, width)
    far = chips - 1
    half_rows = pl.cdiv(pl.cdiv(width // LANES, 2), 16) * 16

    def ahead(i):
        return 0, jnp.minimum(i, chunks - 1)

    def behind(i):
        return 0, jnp.maximum(i - OUT_LAG, 0)

    def ahead_docs(i):
        return jnp.minimum(i, chunks - 1), 0

    def behind_docs(i):
        return jnp.maximum(i - OUT_LAG, 0), 0

    dma = pltpu.SemaphoreType.DMA
    scratch = [
        pltpu.VMEM((terms, score_rows, docs), jnp.float32),
        pltpu.VMEM((blocks * rows + 16, docs), jnp.bfloat16),
        pltpu.VMEM((blocks * rows + 16, docs), jnp.bfloat16),
        pltpu.VMEM((chunks, blocks, rows, width), jnp.bfloat16),
        pltpu.VMEM((chunks, chips, rows, width), jnp.float32),
        pltpu.VMEM((chunks, chips, rows, width), jnp.bfloat16),
        pltpu.VMEM((chunks, chips, rows, width), jnp.bfloat16),
        pltpu.VMEM((chunks, far, rows, width), jnp.bfloat16),
        pltpu.VMEM((chunks, far, rows, width), jnp.bfloat16),
        pltpu.VMEM((chunks, 1, width), jnp.float32),
        pltpu.VMEM((chunks, 1, width), jnp.float32),
        pltpu.VMEM((chunks, 1, width), jnp.float32),
        pltpu.VMEM((chunks, 2, half_rows, LANES), jnp.bfloat16),
        pltpu.VMEM((chunks, far, 2, half_rows, LANES), jnp.bfloat16),
        pltpu.VMEM((2, half_rows, LANES), jnp.float32),
        dma((terms - 1,)), dma((terms - 1,)),
        dma((chunks,)), dma((chunks,)),
        dma((chunks, far)), dma((chunks, far)),
        dma((chunks, far)), dma((chunks, far)),
        dma((chunks,)), dma((chunks,)),
        dma((chunks, far)), dma((chunks, far)),
        dma((chunks,)), dma((chunks,)),
        dma((chunks, far)), dma((chunks, far)),
        dma((chunks, far)), dma((chunks, far)),
        pltpu.VMEM((2, rows, width), jnp.bfloat16),
        pltpu.VMEM((2, width, docs), jnp.bfloat16),
        dma((2,)), dma((2,)),
    ]
    query_grad, doc_grad = pl.pallas_call(
        functools.partial(kernel, chips, terms, chunks, blocks * rows, blocks * docs),
        grid=(chunks + OUT_LAG,),
        out_shape=(
            pltpu.VMEM((chunks, rows, width), jnp.bfloat16),
            pltpu.VMEM((chunks * width, docs), jnp.bfloat16),
        ),
        in_specs=[
            pl.BlockSpec((score_rows, docs), lambda i: (0, 0)),
            pl.BlockSpec((rows, width), ahead),
            pl.BlockSpec((width, docs), ahead_docs),
            pl.BlockSpec((rows, width), behind),
            pl.BlockSpec((width, docs), behind_docs),
        ],
        out_specs=(pl.BlockSpec(memory_space=pl.ANY), pl.BlockSpec(memory_space=pl.ANY)),
        scratch_shapes=scratch,
        compiler_params=pltpu.CompilerParams(
            collective_id=0,
            has_side_effects=True,
            vmem_limit_bytes=46 * 1024 * 1024,
            dimension_semantics=("arbitrary",),
        ),
        cost_estimate=pl.CostEstimate(
            flops=4 * docs * blocks * rows * vocab,
            bytes_accessed=6 * (rows + docs) * vocab,
            transcendentals=(rows + docs) * vocab,
        ),
    )(score_grad, query_logits, doc_logits, query_logits, doc_logits)
    query_grad = query_grad.transpose(1, 0, 2).reshape(rows, chunks * width)[:, :vocab]
    return query_grad, doc_grad[:vocab].T


def solution(mesh):
    placed = (
        P(("grp", "batch", "sub"), "term"),
        P(("grp", "batch", "sub"), "term"),
        P(("grp", "term"), ("batch", "sub")),
    )
    return jax.shard_map(
        functools.partial(on_device, mesh.shape["batch"], mesh.shape["term"]),
        mesh=mesh,
        in_specs=placed,
        out_specs=(P(("grp", "batch", "sub"), "term"), P(("grp", "batch", "sub"), "term")),
        check_vma=False,
    )
```

```python
import functools

import jax
import jax.numpy as jnp
from jax import lax
from jax.experimental import pallas as pl
from jax.experimental.pallas import tpu as pltpu
from jax.sharding import PartitionSpec as P

query_reg = 1.0
doc_reg = 0.6

LANES = 128
CHUNK_TILES = 27
FORWARD_LAG = 2
OUT_LAG = 3
MESH = pl.DeviceIdType.MESH


def impacts(logits):
    return jnp.log1p(jnp.maximum(logits.astype(jnp.float32), 0.0)).astype(jnp.bfloat16)


def saturate_back(grad, logits):
    values = logits.astype(jnp.float32)
    scaled = grad / (1.0 + jnp.maximum(values, 0.0))
    return jnp.where(values > 0.0, scaled, 0.0).astype(jnp.bfloat16)


def kernel(
    chips, terms, chunks, num_queries, num_docs,
    score_ref, q_in, d_in, q_again, d_again, q_out, d_out,
    score_all, score_keep_send, score_rows,
    q_all, p_keep, p_send, p_recv, x_send, x_recv, s_own, s_recv, s_chip, s_pack, s_far, s_rows,
    sc_ss, sc_rs, qs_ss, qs_rs, qx_ss, qx_rs, qf_ss, qf_rs,
    p_ss, p_rs, x_ss, x_rs, s_ss, s_rs, sx_ss, sx_rs, sf_ss, sf_rs,
    q_ring, d_ring, qw_sem, dw_sem,
):
    step = pl.program_id(0)
    rows = q_in.shape[0]
    term = lax.axis_index("term")
    chip = lax.axis_index("batch")
    core = lax.axis_index("sub")
    other = 1 - core
    sibling = {"sub": other}
    block = chip * 2 + core

    def chip_up(k):
        return lax.rem(chip + k, chips)

    def chip_down(k):
        return lax.rem(chip + chips - k, chips)

    def remote(src, dst, send, recv, device):
        return pltpu.make_async_remote_copy(
            src_ref=src, dst_ref=dst, send_sem=send, recv_sem=recv,
            device_id=device, device_id_type=MESH,
        )

    def score_copy(k):
        return remote(
            score_all.at[term], score_all.at[term], sc_ss.at[k - 1], sc_rs.at[k - 1],
            {"term": lax.rem(term + k, terms)},
        )

    def score_arrival(k):
        source = lax.rem(term + terms - k, terms)
        return remote(
            score_all.at[source], score_all.at[source], sc_ss.at[k - 1], sc_rs.at[k - 1],
            {"term": lax.rem(term + k, terms)},
        )

    def q_to_sibling(c):
        return remote(q_all.at[c, block], q_all.at[c, block], qs_ss.at[c], qs_rs.at[c], sibling)

    def q_from_sibling(c):
        at = chip * 2 + other
        return remote(q_all.at[c, at], q_all.at[c, at], qs_ss.at[c], qs_rs.at[c], sibling)

    def q_to_chip(c, k):
        return remote(
            q_all.at[c, block], q_all.at[c, block], qx_ss.at[c, k - 1], qx_rs.at[c, k - 1],
            {"batch": chip_up(k)},
        )

    def q_from_chip(c, k):
        at = chip_down(k) * 2 + core
        return remote(
            q_all.at[c, at], q_all.at[c, at], qx_ss.at[c, k - 1], qx_rs.at[c, k - 1],
            {"batch": chip_up(k)},
        )

    def q_forward(c, k):
        at = chip_down(k) * 2 + core
        return remote(
            q_all.at[c, at], q_all.at[c, at], qf_ss.at[c, k - 1], qf_rs.at[c, k - 1], sibling
        )

    def q_forwarded(c, k):
        at = chip_down(k) * 2 + other
        return remote(
            q_all.at[c, at], q_all.at[c, at], qf_ss.at[c, k - 1], qf_rs.at[c, k - 1], sibling
        )

    def p_copy(c):
        return remote(p_send.at[c], p_recv.at[c], p_ss.at[c], p_rs.at[c], sibling)

    def x_copy(c, k):
        return remote(
            x_send.at[c, k - 1], x_recv.at[c, k - 1], x_ss.at[c, k - 1], x_rs.at[c, k - 1],
            {"batch": chip_up(k)},
        )

    def s_copy(c):
        return remote(s_own.at[c], s_recv.at[c], s_ss.at[c], s_rs.at[c], sibling)

    def sx_copy(c, k):
        return remote(
            s_pack.at[c, core], s_far.at[c, k - 1, core], sx_ss.at[c, k - 1], sx_rs.at[c, k - 1],
            {"batch": chip_up(k)},
        )

    def s_forward(c, k):
        return remote(
            s_far.at[c, k - 1, core], s_far.at[c, k - 1, core],
            sf_ss.at[c, k - 1], sf_rs.at[c, k - 1], sibling,
        )

    def s_forwarded(c, k):
        return remote(
            s_far.at[c, k - 1, other], s_far.at[c, k - 1, other],
            sf_ss.at[c, k - 1], sf_rs.at[c, k - 1], sibling,
        )

    width = q_in.shape[1]
    tiles = width // LANES
    half_tiles = pl.cdiv(tiles, 2)

    def q_write(c):
        slot = lax.rem(c, 2)
        return pltpu.make_async_copy(q_ring.at[slot], q_out.at[c], qw_sem.at[slot])

    def d_write(c):
        slot = lax.rem(c, 2)
        return pltpu.make_async_copy(
            d_ring.at[slot], d_out.at[pl.ds(pl.multiple_of(c * width, LANES), width)], dw_sem.at[slot]
        )

    @pl.when(step == 0)
    def _():
        barrier = pltpu.get_barrier_semaphore()
        pl.semaphore_signal(barrier, inc=1, device_id=sibling, device_id_type=MESH)
        for k in range(1, chips):
            pl.semaphore_signal(barrier, inc=1, device_id={"batch": chip_up(k)}, device_id_type=MESH)
        for k in range(1, terms):
            pl.semaphore_signal(
                barrier, inc=1, device_id={"term": lax.rem(term + k, terms)}, device_id_type=MESH
            )
        pl.semaphore_wait(barrier, 1 + (chips - 1) + (terms - 1))
        s_rows[...] = jnp.zeros_like(s_rows)
        score_all[term] = score_ref[...].astype(jnp.float32)
        for k in range(1, terms):
            score_copy(k).start()

    @pl.when(step < chunks)
    def _():
        c = step
        q_all[c, block] = impacts(q_in[...])
        for k in range(1, chips):
            q_to_chip(c, k).start()
        q_to_sibling(c).start()

    @pl.when(step == 0)
    def _():
        for k in range(1, terms):
            score_arrival(k).wait_recv()
        per = rows // score_all.shape[1]
        docs = score_all.shape[2]

        def score_block(at):
            return score_all[pl.ds(at * per, per)].reshape(rows, docs).astype(jnp.bfloat16)

        for k in range(chips):
            kept = chip_up(k) * 2
            score_keep_send[pl.ds(k * rows, rows), :] = score_block(kept + core)
            score_keep_send[pl.ds((chips + k) * rows, rows), :] = score_block(kept + other)
        ones = jnp.ones((16, docs), jnp.bfloat16)
        score_keep_send[pl.ds(2 * chips * rows, 16), :] = ones
        whole = score_all[...].reshape(2 * chips * rows, docs)
        score_rows[pl.ds(0, 2 * chips * rows), :] = whole.astype(jnp.bfloat16)
        score_rows[pl.ds(2 * chips * rows, 16), :] = ones
        for k in range(1, terms):
            score_copy(k).wait_send()

    @pl.when(step < chunks)
    def _():
        c = step
        half = chips * rows
        partial = lax.dot_general(
            score_keep_send[...], impacts(d_in[...]), (((1,), (1,)), ((), ())),
            preferred_element_type=jnp.float32,
        )
        width = partial.shape[1]
        p_send[c] = partial[half : 2 * half].astype(jnp.bfloat16).reshape(chips, rows, width)
        s_own[c] = partial[2 * half : 2 * half + 1]
        p_copy(c).start()
        s_copy(c).start()
        p_keep[c] = partial[:half].reshape(chips, rows, width)

    @pl.when(jnp.logical_and(step >= 1, step < chunks + 1))
    def _():
        c = step - 1
        p_copy(c).wait_recv()
        s_copy(c).wait_recv()
        chip_sums = s_own[c] + s_recv[c]
        s_chip[c] = chip_sums
        for t in range(tiles):
            h, r = divmod(t, half_tiles)
            s_rows[h, r : r + 1, :] = chip_sums[:, t * LANES : (t + 1) * LANES]
        s_pack[c] = s_rows[...].astype(jnp.bfloat16)
        for k in range(1, chips):
            sx_copy(c, k).start()
        for k in range(1, chips):
            x_send[c, k - 1] = (p_keep[c, k] + p_recv[c, k].astype(jnp.float32)).astype(jnp.bfloat16)
            x_copy(c, k).start()

    @pl.when(jnp.logical_and(step >= FORWARD_LAG, step < chunks + FORWARD_LAG))
    def _():
        c = step - FORWARD_LAG
        for k in range(1, chips):
            q_from_chip(c, k).wait_recv()
            q_forward(c, k).start()
            sx_copy(c, k).wait_recv()
            s_forward(c, k).start()

    @pl.when(step >= OUT_LAG)
    def _():
        c = step - OUT_LAG
        q_from_sibling(c).wait_recv()
        for k in range(1, chips):
            q_forwarded(c, k).wait_recv()
        blocks = q_all.shape[1]
        width = q_all.shape[3]
        all_impacts = q_all[c].reshape(blocks * rows, width)
        query_sums = jnp.dot(
            jnp.ones((16, blocks * rows), jnp.bfloat16), all_impacts,
            preferred_element_type=jnp.float32,
        )[:1]
        doc_sums = s_chip[c]
        for k in range(1, chips):
            s_forwarded(c, k).wait_recv()
            s_rows[...] = s_far[c, k - 1].astype(jnp.float32)
            pieces = []
            for t in range(tiles):
                h, r = divmod(t, half_tiles)
                pieces.append(s_rows[h, r : r + 1, :])
            doc_sums = doc_sums + jnp.concatenate(pieces, axis=1)
        slot = lax.rem(c, 2)

        @pl.when(c >= 2)
        def _():
            q_write(c - 2).wait()
            d_write(c - 2).wait()

        doc_reg_grad = (2.0 * doc_reg / num_docs) * doc_sums
        high = doc_reg_grad.astype(jnp.bfloat16)
        left = doc_reg_grad - high.astype(jnp.float32)
        middle = left.astype(jnp.bfloat16)
        low = (left - middle.astype(jnp.float32)).astype(jnp.bfloat16)
        parts = jnp.concatenate(
            [high, middle, low, jnp.zeros((13, width), jnp.bfloat16)], axis=0
        )
        doc_grad = lax.dot_general(
            jnp.concatenate([all_impacts, parts], axis=0), score_rows[...],
            (((0,), (0,)), ((), ())), preferred_element_type=jnp.float32,
        )
        d_ring[slot] = saturate_back(doc_grad, d_again[...])
        d_write(c).start()
        query_grad = p_keep[c, 0] + p_recv[c, 0].astype(jnp.float32)
        query_grad = query_grad + (2.0 * query_reg / num_queries) * query_sums
        for k in range(1, chips):
            x_copy(c, k).wait_recv()
            query_grad = query_grad + x_recv[c, k - 1].astype(jnp.float32)
        q_ring[slot] = saturate_back(query_grad, q_again[...])
        q_write(c).start()
        q_to_sibling(c).wait_send()
        p_copy(c).wait_send()
        s_copy(c).wait_send()
        for k in range(1, chips):
            q_to_chip(c, k).wait_send()
            q_forward(c, k).wait_send()
            x_copy(c, k).wait_send()
            sx_copy(c, k).wait_send()
            s_forward(c, k).wait_send()

        @pl.when(c == chunks - 1)
        def _():
            for last in range(max(0, chunks - 2), chunks):
                q_write(last).wait()
                d_write(last).wait()


def drain(width, d_from, d_to, d_sem):
    vocab = d_to.shape[0]
    chunks = pl.cdiv(vocab, width)
    copies = []
    for c in range(chunks):
        size = min(width, vocab - c * width)
        part = pl.ds(c * width, size)
        copies.append(pltpu.make_async_copy(d_from.at[part], d_to.at[part], d_sem.at[c]))
    for copy in copies:
        copy.start()
    for copy in copies:
        copy.wait()


def on_device(chips, terms, query_logits, doc_logits, score_grad):
    rows, vocab = query_logits.shape
    docs = doc_logits.shape[0]
    doc_logits = doc_logits.T
    score_rows = score_grad.shape[0]
    blocks = 2 * chips
    tiles = pl.cdiv(vocab, LANES)
    chunks = max(1, round(tiles / CHUNK_TILES))
    width = pl.cdiv(tiles, chunks) * LANES
    chunks = pl.cdiv(vocab, width)
    far = chips - 1
    half_rows = pl.cdiv(pl.cdiv(width // LANES, 2), 16) * 16

    def ahead(i):
        return 0, jnp.minimum(i, chunks - 1)

    def behind(i):
        return 0, jnp.maximum(i - OUT_LAG, 0)

    def ahead_docs(i):
        return jnp.minimum(i, chunks - 1), 0

    def behind_docs(i):
        return jnp.maximum(i - OUT_LAG, 0), 0

    dma = pltpu.SemaphoreType.DMA
    scratch = [
        pltpu.VMEM((terms, score_rows, docs), jnp.float32),
        pltpu.VMEM((blocks * rows + 16, docs), jnp.bfloat16),
        pltpu.VMEM((blocks * rows + 16, docs), jnp.bfloat16),
        pltpu.VMEM((chunks, blocks, rows, width), jnp.bfloat16),
        pltpu.VMEM((chunks, chips, rows, width), jnp.float32),
        pltpu.VMEM((chunks, chips, rows, width), jnp.bfloat16),
        pltpu.VMEM((chunks, chips, rows, width), jnp.bfloat16),
        pltpu.VMEM((chunks, far, rows, width), jnp.bfloat16),
        pltpu.VMEM((chunks, far, rows, width), jnp.bfloat16),
        pltpu.VMEM((chunks, 1, width), jnp.float32),
        pltpu.VMEM((chunks, 1, width), jnp.float32),
        pltpu.VMEM((chunks, 1, width), jnp.float32),
        pltpu.VMEM((chunks, 2, half_rows, LANES), jnp.bfloat16),
        pltpu.VMEM((chunks, far, 2, half_rows, LANES), jnp.bfloat16),
        pltpu.VMEM((2, half_rows, LANES), jnp.float32),
        dma((terms - 1,)), dma((terms - 1,)),
        dma((chunks,)), dma((chunks,)),
        dma((chunks, far)), dma((chunks, far)),
        dma((chunks, far)), dma((chunks, far)),
        dma((chunks,)), dma((chunks,)),
        dma((chunks, far)), dma((chunks, far)),
        dma((chunks,)), dma((chunks,)),
        dma((chunks, far)), dma((chunks, far)),
        dma((chunks, far)), dma((chunks, far)),
        pltpu.VMEM((2, rows, width), jnp.bfloat16),
        pltpu.VMEM((2, width, docs), jnp.bfloat16),
        dma((2,)), dma((2,)),
    ]
    query_grad, doc_grad = pl.pallas_call(
        functools.partial(kernel, chips, terms, chunks, blocks * rows, blocks * docs),
        grid=(chunks + OUT_LAG,),
        out_shape=(
            pltpu.VMEM((chunks, rows, width), jnp.bfloat16),
            pltpu.VMEM((chunks * width, docs), jnp.bfloat16),
        ),
        in_specs=[
            pl.BlockSpec((score_rows, docs), lambda i: (0, 0)),
            pl.BlockSpec((rows, width), ahead),
            pl.BlockSpec((width, docs), ahead_docs),
            pl.BlockSpec((rows, width), behind),
            pl.BlockSpec((width, docs), behind_docs),
        ],
        out_specs=(pl.BlockSpec(memory_space=pl.ANY), pl.BlockSpec(memory_space=pl.ANY)),
        scratch_shapes=scratch,
        compiler_params=pltpu.CompilerParams(
            collective_id=0,
            has_side_effects=True,
            vmem_limit_bytes=46 * 1024 * 1024,
            dimension_semantics=("arbitrary",),
        ),
        cost_estimate=pl.CostEstimate(
            flops=4 * docs * blocks * rows * vocab,
            bytes_accessed=6 * (rows + docs) * vocab,
            transcendentals=(rows + docs) * vocab,
        ),
    )(score_grad, query_logits, doc_logits, query_logits, doc_logits)
    query_grad = query_grad.transpose(1, 0, 2).reshape(rows, chunks * width)[:, :vocab]
    doc_grad = pl.pallas_call(
        functools.partial(drain, width),
        out_shape=jax.ShapeDtypeStruct((vocab, docs), jnp.bfloat16),
        in_specs=[pl.BlockSpec(memory_space=pl.ANY)],
        out_specs=pl.BlockSpec(memory_space=pl.ANY),
        scratch_shapes=[dma((chunks,))],
        compiler_params=pltpu.CompilerParams(vmem_limit_bytes=4 * 1024 * 1024),
    )(doc_grad)
    return query_grad, doc_grad.T


def solution(mesh):
    placed = (
        P(("grp", "batch", "sub"), "term"),
        P(("grp", "batch", "sub"), "term"),
        P(("grp", "term"), ("batch", "sub")),
    )
    return jax.shard_map(
        functools.partial(on_device, mesh.shape["batch"], mesh.shape["term"]),
        mesh=mesh,
        in_specs=placed,
        out_specs=(P(("grp", "batch", "sub"), "term"), P(("grp", "batch", "sub"), "term")),
        check_vma=False,
    )
```
